32 devices in a mesh: dp: 4 (over y, x), modes: 8 (over z, core).
Axes of the slice: x: 2, y: 2, z: 4, core: 2. Of those that a mesh axis runs over, the one named last changes fastest.
Arguments:
- patches: bfloat16 [4, 4, 8, 512, 768], P(None, 'dp', 'modes'), may hold values from -6 to 6
- cotangent: bfloat16 [4, 4, 8, 512, 768], P(None, 'dp', 'modes'), may hold values from -6 to 6
- heights: int32 [4, 4], P(None, 'dp'), may hold values from 2 to 8, as said below
- widths: int32 [4, 4], P(None, 'dp'), may hold values from 256 to 512, as said below
- band_lengths: int32 [8], replicated, may hold values from 1 to 64, as said below
- dense_master: float32 [3072, 2, 768], P(('dp', 'modes'))
- dense_first: float32 [3072, 2, 768], P(('dp', 'modes')), may hold values from -0.00030517578 to 0.00030517578
- dense_second: float32 [3072, 2, 768], P(('dp', 'modes')), may hold values from 5.1756865e-09 to 8.360725e-08
- spectral_master: float32 [2, 2, 8, 96, 96], replicated, may hold values from -0.4375 to 0.4375
- spectral_first: float32 [2, 2, 8, 96, 96], replicated, may hold values from -0.00030517578 to 0.00030517578
- spectral_second: float32 [2, 2, 8, 96, 96], replicated, may hold values from 5.1756865e-09 to 8.360725e-08
- vector_master: float32 [13, 768], replicated, may hold values from -1 to 2
- vector_first: float32 [13, 768], replicated, may hold values from -0.0008544922 to 0.0008544922
- vector_second: float32 [13, 768], replicated, may hold values from 4.5784923e-08 to 7.564465e-07
Outputs:
- output: bfloat16 [4, 4, 8, 512, 768], P(None, 'dp', 'modes')
- input_grad: bfloat16 [4, 4, 8, 512, 768], P(None, 'dp', 'modes')
- grad_norm: float32 [], replicated
- dense_grad: float32 [3072, 2, 768], P(('dp', 'modes'))
- dense_new: float32 [3072, 2, 768], P(('dp', 'modes'))
- dense_first_new: float32 [3072, 2, 768], P(('dp', 'modes'))
- dense_second_new: float32 [3072, 2, 768], P(('dp', 'modes'))
- spectral_grad: float32 [2, 2, 8, 96, 96], replicated
- spectral_new: float32 [2, 2, 8, 96, 96], replicated
- spectral_first_new: float32 [2, 2, 8, 96, 96], replicated
- spectral_second_new: float32 [2, 2, 8, 96, 96], replicated
- vector_grad: float32 [13, 768], replicated
- vector_new: float32 [13, 768], replicated
- vector_first_new: float32 [13, 768], replicated
- vector_second_new: float32 [13, 768], replicated
The draws below stay inside these ranges and needn't reach their ends.
Inputs may be any that keep to these rules, and one draw needn't show every extreme that they name: `heights`: among the entries of one index of dp over all micro-batches, one is exactly 8. `widths`: among the entries of one index of dp over all micro-batches, one is exactly 512. `band_lengths`: band j holds the wavenumbers from the sum of the earlier lengths on; one length is exactly 64; the lengths may add up to more than 256 or to less.
All inputs are finite; a program needn't handle non-finite values.
Results may differ from the reference program's by a relative error of at most 0.015.
The reference program's roundings to bfloat16 on the way count: a program that leaves them out, or rounds other values in their place, can miss the bound.
Values may be sent and summed in bfloat16 or wider, within the bound.
No kernel may reach another device: no remote copies, remote signals or barrier semaphores. Data moves between devices by JAX's collectives and lax.ppermute only.
A program may use at most 384 MiB of HBM per device.

```python
import math
import jax
import jax.numpy as jnp
from jax import lax

D = 768
FF = 3072
NB = 8
BS = 96
WB = 512
MICRO = 4
CROPS = 1
STEP = 10
HB = 8
MAXB = 64
BANDS = 8
CROPS_ALL = 4


def forced_entries(key, lowest, highest):
    value_key, pick_key = jax.random.split(key)
    values = jax.random.randint(value_key, (MICRO, CROPS_ALL), lowest, highest + 1)
    group_count = CROPS_ALL // CROPS
    chosen = jax.random.randint(pick_key, (group_count,), 0, MICRO * CROPS)
    micro_pos = jnp.arange(MICRO, dtype=jnp.int32)[:, None]
    columns = jnp.arange(CROPS_ALL, dtype=jnp.int32)[None, :]
    local_pos = micro_pos * CROPS + columns % CROPS
    hit = local_pos == chosen[columns // CROPS]
    return jnp.where(hit, highest, values).astype(jnp.int32)


def draw_heights(key, part):
    key = jax.random.fold_in(key, 11)
    return forced_entries(key, max(1, HB // 4), HB)


def draw_widths(key, part):
    key = jax.random.fold_in(key, 12)
    return forced_entries(key, WB // 2, WB)


def draw_band_lengths(key, part):
    key = jax.random.fold_in(key, 13)
    one_key, two_key, pick_key, regime_key, upper_key = jax.random.split(key, 5)
    first_draw = jax.random.randint(one_key, (BANDS,), 0, MAXB)
    second_draw = jax.random.randint(two_key, (BANDS,), 0, MAXB)
    short_lengths = 1 + jnp.minimum(first_draw, second_draw)
    long_lengths = jax.random.randint(upper_key, (BANDS,), MAXB // 2, MAXB + 1)
    regime = jax.random.randint(regime_key, (), 0, 2)
    lengths = jnp.where(regime == 1, long_lengths, short_lengths)
    chosen = jax.random.randint(pick_key, (), 0, BANDS)
    return jnp.where(jnp.arange(BANDS, dtype=jnp.int32) == chosen, MAXB, lengths).astype(jnp.int32)


def draw_dense_master(key, part):
    key = jax.random.fold_in(key, 17)
    growth = math.log(3.0)
    normal_base = jax.random.truncated_normal(key, -4.0, 4.0, (FF, 2, D), jnp.float32)
    position = jnp.arange(FF, dtype=jnp.float32) / (FF - 1) - 0.5
    row_scale = jnp.exp(growth * position)[:, None, None]
    fan_scale = jnp.array([D ** (-0.5), FF ** (-0.5)], jnp.float32)[None, :, None]
    return normal_base * row_scale * fan_scale


def draw_vector_master(key, part):
    key = jax.random.fold_in(key, 19)
    normal_base = 0.2 * jax.random.truncated_normal(key, -4.0, 4.0, (13, D), jnp.float32)
    row_index = jnp.arange(13, dtype=jnp.int32)
    gain_lift = ((row_index % 2 == 0) & (row_index < 4)).astype(jnp.float32)[:, None]
    return normal_base + gain_lift


def steps_of(key, extent, shards, smallest, largest):
    def one(dim, parts):
        draws = jax.random.uniform(jax.random.fold_in(jax.random.fold_in(key, 6), dim), (parts,), jnp.float32, smallest / len(shards), largest / len(shards))
        return jnp.repeat(jnp.exp(draws), extent[dim] // parts).reshape((-1,) + (1,) * (len(extent) - dim - 1))

    level = one(*shards[0])
    for cut in shards[1:]:
        level = level * one(*cut)
    return level


def centred(stream_key, shape, scale, most, pieces=(), kind=jnp.bfloat16):
    drawn = jax.random.normal(stream_key, shape, jnp.float32) * scale
    if len(pieces) > 0:
        drawn = steps_of(stream_key, shape, pieces, -0.22, 0.18) * drawn
    return jnp.clip(drawn, min=-most, max=most).astype(kind)


def setup_inputs(seed: int = 0) -> dict:
    key_list = jax.random.split(jax.random.key(seed), 15)
    return {
        "patches": centred(key_list[0], (MICRO, CROPS_ALL, HB, WB, D), 1.0, 6.0, ((1, 4), (2, 8))),
        "cotangent": centred(key_list[1], (MICRO, CROPS_ALL, HB, WB, D), 1.0, 6.0, ((1, 4), (2, 8))),
        "heights": draw_heights(jax.random.fold_in(key_list[14], 71), 0),
        "widths": draw_widths(jax.random.fold_in(key_list[14], 71), 0),
        "band_lengths": draw_band_lengths(jax.random.fold_in(key_list[14], 71), 0),
        "dense_master": draw_dense_master(jax.random.fold_in(key_list[14], 71), 0),
        "dense_first": centred(key_list[6], (FF, 2, D), (81 * (2 * FF * D + 4 * NB * BS * BS + 13 * D)) ** -0.5, 0.00030517578, ((0, 32),), jnp.float32),
        "dense_second": jnp.clip(jnp.exp(math.log(8.360724734757241e-08) - 2.7821582 * jax.random.uniform(key_list[7], (FF, 2, D), jnp.float32) ** steps_of(key_list[7], (FF, 2, D), ((0, 32),), -0.2, 0.2)), 5.175686546010638e-09, 8.360724734757241e-08),
        "spectral_master": centred(key_list[8], (2, 2, NB, BS, BS), (2 * BS) ** -0.5, 0.4375, (), jnp.float32),
        "spectral_first": centred(key_list[9], (2, 2, NB, BS, BS), (81 * (2 * FF * D + 4 * NB * BS * BS + 13 * D)) ** -0.5, 0.00030517578, (), jnp.float32),
        "spectral_second": jnp.clip(jnp.exp(jax.random.uniform(key_list[10], (2, 2, NB, BS, BS), jnp.float32, math.log(5.175686546010638e-09), math.log(8.360724734757241e-08))), 5.175686546010638e-09, 8.360724734757241e-08),
        "vector_master": draw_vector_master(jax.random.fold_in(key_list[14], 71), 0),
        "vector_first": centred(key_list[12], (13, D), (9 * (2 * FF * D + 4 * NB * BS * BS + 13 * D)) ** -0.5, 0.0008544922, (), jnp.float32),
        "vector_second": jnp.clip(jnp.exp(jax.random.uniform(key_list[13], (13, D), jnp.float32, math.log(4.5784922519942484e-08), math.log(7.56446524974308e-07))), 4.5784922519942484e-08, 7.56446524974308e-07),
    }


PRECISE = lax.Precision.HIGHEST
SHRINK_LEVEL = 0.01
NORM_EPS = 1e-05
CLIP_LEVEL = 1.0
BETA_FIRST = 0.9
BETA_SECOND = 0.95
ADAM_EPS = 1e-08
RATE_MATRIX = 0.05
RATE_VECTOR = 0.5
DECAY_MATRIX = 0.1

@jax.custom_vjp
def low(v):
    return lax.optimization_barrier(v.astype(jnp.bfloat16)).astype(jnp.float32)

@jax.custom_vjp
def low_back(v):
    return v

def low_keep(v):
    return (low(v), None)

def low_pass(kept, grad):
    return (grad,)

def back_keep(v):
    return (v, None)

def back_low(kept, grad):
    return (low(grad),)
low.defvjp(low_keep, low_pass)
low_back.defvjp(back_keep, back_low)

def wave_table(wavenumbers, length, factors):
    positions = jnp.arange(length, dtype=jnp.int32)
    phase_int = wavenumbers[:, None] * positions[None, :] % length
    angles = phase_int.astype(jnp.float32) * (2.0 * math.pi / length)
    return jnp.stack([jnp.cos(angles) * factors[:, None], -jnp.sin(angles) * factors[:, None]])

def row_tables(length):
    row_index = jnp.arange(length, dtype=jnp.int32)
    phase_int = row_index[:, None] * row_index[None, :] % length
    angles = phase_int.astype(jnp.float32) * (2.0 * math.pi / length)
    cosine = jnp.cos(angles)
    sines = jnp.sin(angles)
    forward = jnp.stack([jnp.stack([cosine, sines], axis=1), jnp.stack([-sines, cosine], axis=1)])
    inverse = jnp.stack([jnp.stack([cosine, -sines], axis=1), jnp.stack([sines, cosine], axis=1)])
    return (forward, inverse)

def complex_matrix(weights):
    return jnp.stack([jnp.stack([weights[0], weights[1]]), jnp.stack([-weights[1], weights[0]])])

def mix_ref(values, matrix):
    full_shape = values.shape
    blocked = values.reshape(full_shape[:-1] + (NB, BS))
    mixed = jnp.einsum('pabni,pqnij->qabnj', blocked, matrix, precision=PRECISE)
    return mixed.reshape(full_shape)

def shrink(values):
    return values - SHRINK_LEVEL * jnp.tanh(values / SHRINK_LEVEL)

def norm_rows(values, gain_row, shift_row):
    centered = values - lax.optimization_barrier(jnp.mean(values, axis=-1, keepdims=True))
    return centered * lax.rsqrt(lax.optimization_barrier(jnp.mean(centered * centered, axis=-1, keepdims=True)) + NORM_EPS) * gain_row + shift_row

def adam_update(master, first_old, second_old, gradient, rate, decay):
    first_new = BETA_FIRST * first_old + (1.0 - BETA_FIRST) * gradient
    second_new = BETA_SECOND * second_old + (1.0 - BETA_SECOND) * gradient * gradient
    moved = first_new / (1.0 - BETA_FIRST ** STEP) / (jnp.sqrt(second_new / (1.0 - BETA_SECOND ** STEP)) + ADAM_EPS)
    return (master - rate * (moved + decay * master), first_new, second_new)

def reference(patches, cotangent, heights, widths, band_lengths, dense_master, dense_first, dense_second, spectral_master, spectral_first, spectral_second, vector_master, vector_first, vector_second):
    wave_count = WB // 2
    ortho_scale = (HB * WB) ** (-0.5)
    wavenumbers = jnp.arange(wave_count, dtype=jnp.int32)
    forward_table = low(wave_table(wavenumbers, WB, jnp.full((wave_count,), ortho_scale, jnp.float32)))
    inverse_table = low(wave_table(wavenumbers, WB, jnp.where(wavenumbers == 0, ortho_scale, 2.0 * ortho_scale)))
    row_forward, row_inverse = row_tables(HB)
    row_forward = low(row_forward)
    row_inverse = low(row_inverse)
    kept_count = jnp.minimum(jnp.sum(band_lengths), wave_count)
    keep_mask = (wavenumbers < kept_count).astype(jnp.float32)[None, None, :, None]

    def crop_forward(cells, cell_mask, dense, spectral, vector):
        masked_in = cells * cell_mask
        normed = norm_rows(masked_in, vector[0], vector[1]) * cell_mask
        narrow = low(normed)
        spread = jnp.einsum('pkw,hwd->phkd', forward_table, narrow, precision=PRECISE)
        spread = low(low_back(spread))
        mode_rows = jnp.einsum('pjqh,qhkd->pjkd', row_forward, spread, precision=PRECISE)
        mode_rows = low(low_back(mode_rows))
        spectral_low = low(spectral)
        pre_active = low_back(mix_ref(mode_rows, complex_matrix(spectral_low[0]))) + vector[4:6][:, None, None, :]
        active = low(jax.nn.gelu(pre_active))
        pre_shrink = low_back(mix_ref(active, complex_matrix(spectral_low[1]))) + vector[6:8][:, None, None, :]
        shrunk = low(shrink(pre_shrink) * keep_mask)
        back_rows = jnp.einsum('phqj,qjkd->phkd', row_inverse, shrunk, precision=PRECISE)
        back_rows = low(low_back(back_rows))
        filtered = low_back(jnp.einsum('pkw,phkd->hwd', inverse_table, back_rows, precision=PRECISE))
        middle = masked_in + normed + filtered
        tokens = low(norm_rows(middle, vector[2], vector[3])).reshape(-1, D)
        dense_low = low(dense)
        upper_in = low_back(jnp.dot(tokens, dense_low[:, 0, :].T, precision=PRECISE)) + vector[9:13].reshape(-1)
        hidden = low(jax.nn.gelu(upper_in))
        lower_out = low_back(jnp.dot(hidden, dense_low[:, 1, :], precision=PRECISE)) + vector[8]
        return (middle + lower_out.reshape(middle.shape)) * cell_mask
    crop_total = MICRO * CROPS_ALL
    heights_flat = heights.reshape(-1)
    widths_flat = widths.reshape(-1)
    row_ok = jnp.arange(HB, dtype=jnp.int32)[None, :, None] < heights_flat[:, None, None]
    col_ok = jnp.arange(WB, dtype=jnp.int32)[None, None, :] < widths_flat[:, None, None]
    masks_all = (row_ok & col_ok).astype(jnp.float32)[..., None]

    def crop_step(totals, crop_items):
        crop_cells, crop_grad, cell_mask = crop_items

        def crop_apply(cells, dense, spectral, vector):
            return crop_forward(cells, cell_mask, dense, spectral, vector)
        result, pullback = jax.vjp(crop_apply, crop_cells.astype(jnp.float32), dense_master, spectral_master, vector_master)
        pulled = pullback(crop_grad.astype(jnp.float32))
        totals = (totals[0] + pulled[1], totals[1] + pulled[2], totals[2] + pulled[3])
        return (totals, (result.astype(jnp.bfloat16), pulled[0].astype(jnp.bfloat16)))
    start_totals = (jnp.zeros_like(dense_master), jnp.zeros_like(spectral_master), jnp.zeros_like(vector_master))
    totals, results = lax.scan(crop_step, start_totals, (patches.reshape(crop_total, HB, WB, D), cotangent.reshape(crop_total, HB, WB, D), masks_all))
    output = results[0].reshape(MICRO, CROPS_ALL, HB, WB, D)
    input_grad = results[1].reshape(MICRO, CROPS_ALL, HB, WB, D)
    dense_sum, spectral_sum, vector_sum = totals
    squares = jnp.sum(dense_sum * dense_sum) + jnp.sum(spectral_sum * spectral_sum) + jnp.sum(vector_sum * vector_sum)
    grad_norm = jnp.sqrt(squares)
    clip_factor = jnp.minimum(1.0, CLIP_LEVEL / (grad_norm + 1e-06))
    dense_grad = dense_sum * clip_factor
    spectral_grad = spectral_sum * clip_factor
    vector_grad = vector_sum * clip_factor
    dense_new, dense_first_new, dense_second_new = adam_update(dense_master, dense_first, dense_second, dense_grad, RATE_MATRIX, DECAY_MATRIX)
    spectral_new, spectral_first_new, spectral_second_new = adam_update(spectral_master, spectral_first, spectral_second, spectral_grad, RATE_MATRIX, DECAY_MATRIX)
    vector_new, vector_first_new, vector_second_new = adam_update(vector_master, vector_first, vector_second, vector_grad, RATE_VECTOR, 0.0)
    return (output, input_grad, grad_norm, dense_grad, dense_new, dense_first_new, dense_second_new, spectral_grad, spectral_new, spectral_first_new, spectral_second_new, vector_grad, vector_new, vector_first_new, vector_second_new)
```

```python
import functools
import math

import jax
import jax.numpy as jnp
import ml_dtypes
import numpy as np
from jax import lax
from jax.experimental import pallas as pl
from jax.experimental.pallas import tpu as pltpu
from jax.sharding import PartitionSpec as P

NB = 8
BS = 96
STEP = 10

SHRINK_LEVEL = 0.01
NORM_EPS = 1e-05
CLIP_LEVEL = 1.0
BETA_FIRST = 0.9
BETA_SECOND = 0.95
ADAM_EPS = 1e-08
RATE_MATRIX = 0.05
RATE_VECTOR = 0.5
DECAY_MATRIX = 0.1

GELU_SCALE = math.sqrt(2.0 / math.pi)
GELU_CUBE = 0.044715
SPAN = 384
LANES = 128
VMEM = 63 * 2**20
SMALL = 24 * 2**20
F32 = jnp.float32
BF16 = jnp.bfloat16


def wave_tables(band_count, row_cells):
    wave_count = row_cells // 2
    slots = wave_count // band_count
    scale = (band_count * row_cells) ** (-0.5)
    waves = np.arange(wave_count)
    phase = (waves[:, None] * np.arange(row_cells)[None, :]) % row_cells
    angle = phase * (2.0 * math.pi / row_cells)
    factor = np.where(waves == 0, scale, 2.0 * scale)[:, None]

    def order(parts):
        parts = np.stack(parts).astype(np.float32).astype(ml_dtypes.bfloat16)
        parts = parts.reshape(2, band_count, slots, row_cells).transpose(1, 0, 2, 3)
        return np.ascontiguousarray(parts.reshape(2 * wave_count, row_cells))

    forward = order([np.cos(angle) * scale, -np.sin(angle) * scale])
    inverse = order([np.cos(angle) * factor, -np.sin(angle) * factor])
    return (
        jnp.asarray(forward),
        jnp.asarray(np.ascontiguousarray(forward.T)),
        jnp.asarray(inverse),
        jnp.asarray(np.ascontiguousarray(inverse.T)),
    )


def row_tables(length):
    row_index = jnp.arange(length, dtype=jnp.int32)
    phase_int = row_index[:, None] * row_index[None, :] % length
    angles = phase_int.astype(F32) * (2.0 * math.pi / length)
    cosine = jnp.cos(angles)
    sines = jnp.sin(angles)
    forward = jnp.stack([jnp.stack([cosine, sines], axis=1), jnp.stack([-sines, cosine], axis=1)])
    inverse = jnp.stack([jnp.stack([cosine, -sines], axis=1), jnp.stack([sines, cosine], axis=1)])
    return (forward.astype(BF16), inverse.astype(BF16))


def norm_forward(values):
    centered = values - jnp.mean(values, axis=-1, keepdims=True)
    factor = lax.rsqrt(jnp.mean(centered * centered, axis=-1, keepdims=True) + NORM_EPS)
    return (centered * factor, factor)


def norm_backward(grad_rows, unit_rows, factor, gain_row):
    scaled = grad_rows * gain_row
    return factor * (
        scaled
        - jnp.mean(scaled, axis=-1, keepdims=True)
        - unit_rows * jnp.mean(scaled * unit_rows, axis=-1, keepdims=True)
    )


def gelu_pair(values):
    square = values * values
    bend = jnp.tanh(values * (GELU_SCALE + (GELU_SCALE * GELU_CUBE) * square))
    half = 0.5 + 0.5 * bend
    slope = GELU_SCALE + (3.0 * GELU_SCALE * GELU_CUBE) * square
    return (values * half, half + (0.5 * values) * (1.0 - bend * bend) * slope)


def gelu_only(values):
    square = values * values
    bend = jnp.tanh(values * (GELU_SCALE + (GELU_SCALE * GELU_CUBE) * square))
    return values * (0.5 + 0.5 * bend)


def dot(left, right):
    return lax.dot_general(left, right, (((1,), (0,)), ((), ())), preferred_element_type=F32)


def dot_nt(left, right):
    return lax.dot_general(left, right, (((1,), (1,)), ((), ())), preferred_element_type=F32)


def dot_tn(left, right):
    return lax.dot_general(left, right, (((0,), (0,)), ((), ())), preferred_element_type=F32)


def adam_update(master, first_old, second_old, gradient, rate, decay):
    first_new = BETA_FIRST * first_old + (1.0 - BETA_FIRST) * gradient
    second_new = BETA_SECOND * second_old + (1.0 - BETA_SECOND) * gradient * gradient
    moved = (
        first_new
        / (1.0 - BETA_FIRST**STEP)
        / (jnp.sqrt(second_new / (1.0 - BETA_SECOND**STEP)) + ADAM_EPS)
    )
    return (master - rate * (moved + decay * master), first_new, second_new)


def valid_rows(count, rows):
    return lax.broadcasted_iota(jnp.int32, (rows, 1), 0) < count


def only(mask, values):
    return jnp.where(mask, values, 0.0)


def params(limit=VMEM):
    return pltpu.CompilerParams(vmem_limit_bytes=limit)


def cost(flops, moved, transcendentals=0):
    return pl.CostEstimate(
        flops=int(flops), bytes_accessed=int(moved), transcendentals=int(transcendentals)
    )


SMEM = pl.BlockSpec(memory_space=pltpu.SMEM)
ANY = pl.BlockSpec(memory_space=pl.ANY)
HBM = pl.BlockSpec(memory_space=pltpu.HBM)
VMEMS = pl.BlockSpec(memory_space=pltpu.VMEM)


def whole(array):
    zeros = (0,) * len(array.shape)
    return pl.BlockSpec(array.shape, lambda *_: zeros)


def tie(values, *ahead):
    return pl.pallas_call(
        lambda *_: None,
        in_specs=[HBM] * (1 + len(ahead)),
        out_specs=HBM,
        out_shape=jax.ShapeDtypeStruct(values.shape, values.dtype),
        input_output_aliases={0: 0},
        compiler_params=params(),
        name="tie",
    )(values, *ahead)


def swap(values, axis, mask):
    count = lax.axis_size(axis)
    return lax.ppermute(values, axis, [(i, i ^ mask) for i in range(count)])


def pick_call(kernel, shapes, *operands, name):
    return pl.pallas_call(
        kernel,
        out_shape=shapes,
        compiler_params=params(),
        cost_estimate=cost(0, 4 * sum(o.size for o in operands)),
        name=name,
    )(*operands)


def chunks_by_mask(values, count, index_of):
    shape = jax.ShapeDtypeStruct(values[0].shape[1:], values[0].dtype)

    def kernel(*refs):
        index = index_of()
        for s, out in enumerate(refs[len(values) :]):
            total = refs[0][pl.ds(index ^ s, 1)]
            for ref in refs[1 : len(values)]:
                total = total + ref[pl.ds(index ^ s, 1)]
            out[...] = total[0]

    return list(pick_call(kernel, [shape] * count, *values, name="sum_and_cut"))


def place_by_mask(parts, index_of):
    shape = jax.ShapeDtypeStruct((len(parts),) + parts[0].shape, parts[0].dtype)

    def kernel(*refs):
        index = index_of()
        for s, ref in enumerate(refs[:-1]):
            refs[-1][pl.ds(index ^ s, 1)] = ref[...][None]

    return pick_call(kernel, shape, *parts, name="place_blocks")


def dp_index():
    return lax.axis_index("dp")


def z_index():
    return lax.axis_index("modes") // 2


def scatter_spectral(keep, send):
    parts = chunks_by_mask([keep, swap(send, "modes", 1)], 4, dp_index)
    parts = parts[:1] + [swap(parts[s], "dp", s) for s in range(1, 4)]
    return chunks_by_mask(parts, 4, z_index)


def own_spectral(parts):
    own = parts[0] + swap(parts[1], "modes", 2)
    return own + (swap(parts[2], "modes", 4) + swap(parts[3], "modes", 6))


def gather_spectral(own, ahead):
    blocks = place_by_mask([tie(own, ahead)] + [swap(own, "modes", 2 * s) for s in range(1, 4)], z_index)
    blocks = place_by_mask([blocks] + [swap(blocks, "dp", s) for s in range(1, 4)], dp_index)
    return (blocks, swap(blocks, "modes", 1))


def sum_four(values, axis, stride):
    one, two, three = (swap(values, axis, s * stride) for s in (1, 2, 3))
    return (values + one) + (two + three)


def row_transform(real, imag, sign):
    diagonal = float(ml_dtypes.bfloat16(math.cos(math.pi / 4)))

    def turn(re, im):
        return (-im, re) if sign > 0 else (im, -re)

    def four(index):
        re = [real[i] for i in index]
        im = [imag[i] for i in index]
        sum_even = (re[0] + re[2], im[0] + im[2])
        gap_even = (re[0] - re[2], im[0] - im[2])
        sum_odd = (re[1] + re[3], im[1] + im[3])
        gap_odd = turn(re[1] - re[3], im[1] - im[3])
        return [
            (sum_even[0] + sum_odd[0], sum_even[1] + sum_odd[1]),
            (gap_even[0] + gap_odd[0], gap_even[1] + gap_odd[1]),
            (sum_even[0] - sum_odd[0], sum_even[1] - sum_odd[1]),
            (gap_even[0] - gap_odd[0], gap_even[1] - gap_odd[1]),
        ]

    even = four((0, 2, 4, 6))
    odd = four((1, 3, 5, 7))
    re, im = odd[1]
    side = turn(re, im)
    odd[1] = (diagonal * (re + side[0]), diagonal * (im + side[1]))
    odd[2] = turn(*odd[2])
    re, im = odd[3]
    side = turn(re, im)
    odd[3] = (diagonal * (side[0] - re), diagonal * (side[1] - im))
    out = [(e[0] + o[0], e[1] + o[1]) for e, o in zip(even, odd)]
    out += [(e[0] - o[0], e[1] - o[1]) for e, o in zip(even, odd)]
    return ([v[0] for v in out], [v[1] for v in out])


def tiles(slots, features):
    for row in range(0, slots, 16):
        for lane in range(0, features, LANES):
            yield row, lane, lane // SPAN, lane % SPAN


def rows_to_modes(rows_ref, modes_ref, first, slots, features):
    for row, lane, group, inner in tiles(slots, features):
        parts = [
            [
                rows_ref[h, p * slots + row : p * slots + row + 16, lane : lane + LANES].astype(F32)
                for h in range(8)
            ]
            for p in range(2)
        ]
        done = row_transform(parts[0], parts[1], -1)
        for p in range(2):
            for j in range(8):
                at = first + j * slots + row
                modes_ref[
                    group, at : at + 16, p * SPAN + inner : p * SPAN + inner + LANES
                ] = done[p][j].astype(modes_ref.dtype)


def modes_to_rows(modes_ref, rows_ref, first, slots, features):
    for row, lane, group, inner in tiles(slots, features):
        parts = [
            [
                modes_ref[
                    group,
                    first + j * slots + row : first + j * slots + row + 16,
                    p * SPAN + inner : p * SPAN + inner + LANES,
                ].astype(F32)
                for j in range(8)
            ]
            for p in range(2)
        ]
        done = row_transform(parts[0], parts[1], 1)
        for p in range(2):
            for h in range(8):
                rows_ref[
                    h, p * slots + row : p * slots + row + 16, lane : lane + LANES
                ] = done[p][h].astype(rows_ref.dtype)


def spread_kernel(first, heights, widths, patches, table, vectors, out, base):
    micro = first + pl.program_id(0)
    count = jnp.where(lax.axis_index("modes") < heights[micro], widths[micro], 0)
    mask = valid_rows(count, patches.shape[0])
    masked_in = only(mask, patches[...].astype(F32))
    unit, _ = norm_forward(masked_in)
    normed = only(mask, unit * vectors[0:1, :] + vectors[1:2, :])
    base[...] = masked_in + normed
    out[...] = dot(table[...], normed.astype(BF16)).astype(BF16).reshape(out.shape)


def mix_kernel(spectral, out):
    blocks = SPAN // BS
    row = lax.broadcasted_iota(jnp.int32, (BS, SPAN), 0)
    column = lax.broadcasted_iota(jnp.int32, (BS, SPAN), 1)
    for group in range(NB // blocks):
        for n in range(blocks):
            place = (column == row + n * BS).astype(F32).astype(BF16)
            re = dot(spectral[0, group * blocks + n].astype(BF16), place)
            im = dot(spectral[1, group * blocks + n].astype(BF16), place)
            top, low = n * BS, SPAN + n * BS
            out[group, top : top + BS, 0:SPAN] = re.astype(BF16)
            out[group, top : top + BS, SPAN:] = im.astype(BF16)
            out[group, low : low + BS, 0:SPAN] = (-im).astype(BF16)
            out[group, low : low + BS, SPAN:] = re.astype(BF16)


def keep_column(limits, slots, rows, micros):
    wave = limits[micros] + lax.broadcasted_iota(jnp.int32, (rows, 1), 0) % slots
    return (wave < limits[micros + 1]).astype(F32)


def filter_kernel(slots, micros, limits, received, mix, bias, modes, back, shrunk):
    features = received.shape[-1]
    crops, size = received.shape[1], 8 * slots
    keep = keep_column(limits, slots, modes.shape[1], micros)
    for crop in range(crops):
        rows_to_modes(received.at[:, crop], modes, crop * size, slots, features)
    for group in range(features // SPAN):
        pre_active = dot(modes[group], mix[0, group]) + bias[0, group]
        active = gelu_only(pre_active).astype(BF16)
        pre_shrink = dot(active, mix[1, group]) + bias[1, group]
        value = pre_shrink - SHRINK_LEVEL * jnp.tanh(pre_shrink * (1.0 / SHRINK_LEVEL))
        shrunk[group] = (keep * value).astype(BF16)
    for crop in range(crops):
        modes_to_rows(shrunk, back.at[:, crop], crop * size, slots, features)


def filter_back_kernel(slots, micros, limits, received, modes, mix, bias, *rest):
    spread, sums, mine, other, full, turned = rest[-6:]
    before = rest[:-6]
    features = received.shape[-1]
    crops, size = received.shape[1], 8 * slots
    keep = keep_column(limits, slots, modes.shape[1], micros)
    for crop in range(crops):
        rows_to_modes(received.at[:, crop], turned, crop * size, slots, features)
    for group in range(features // SPAN):
        pre_active = dot(modes[group], mix[0, group]) + bias[0, group]
        value, slope = gelu_pair(pre_active)
        active = value.astype(BF16)
        pre_shrink = dot(active, mix[1, group]) + bias[1, group]
        bend = jnp.tanh(pre_shrink * (1.0 / SHRINK_LEVEL))
        grad_shrink = turned[group] * (keep * bend * bend)
        shrink_low = grad_shrink.astype(BF16)
        grad_first = dot_nt(shrink_low, mix[1, group]) * slope
        first_low = grad_first.astype(BF16)
        sums[group, 0:1, :] = jnp.sum(grad_first, axis=0, keepdims=True)
        sums[group, 1:2, :] = jnp.sum(grad_shrink, axis=0, keepdims=True)
        full[0, group] = dot_tn(modes[group], first_low)
        full[1, group] = dot_tn(active, shrink_low)
        turned[group] = dot_nt(first_low, mix[0, group]).astype(BF16).astype(F32)
    for crop in range(crops):
        modes_to_rows(turned, spread.at[:, crop], crop * size, slots, features)

    blocks = SPAN // BS
    for layer in range(2):
        for group in range(features // SPAN):
            for n in range(blocks):
                top = slice(n * BS, n * BS + BS)
                low = slice(SPAN + n * BS, SPAN + n * BS + BS)
                re = full[layer, group, top, 0:SPAN] + full[layer, group, low, SPAN:]
                im = full[layer, group, top, SPAN:] - full[layer, group, low, 0:SPAN]
                block = group * blocks + n
                for part, grad in enumerate((re, im)):
                    grad = grad[:, n * BS : n * BS + BS]
                    row, column = layer * 2 + part, block // 2
                    for at, out in enumerate((mine, other)):

                        @pl.when(lax.axis_index("modes") % 2 == (block + at) % 2)
                        def _():
                            if before:
                                out[row, column] = grad + before[at][row, column]
                            else:
                                out[row, column] = grad


def dense_kernel(
    first,
    limits,
    base,
    cotangent,
    back,
    inverse_turned,
    inverse,
    vectors,
    hidden_bias,
    mine,
    other,
    *rest,
):
    output, hidden, upper, tokens, grad_low, grad_back, middle, sums, upper_sums = rest[-13:-4]
    lower, grad_tokens, units, factors = rest[-4:]
    step, steps = pl.program_id(1), pl.num_programs(1)
    mask = valid_rows(limits[first + pl.program_id(0)], base.shape[0])

    @pl.when(step == 0)
    def _():
        total = base[...] + dot(inverse_turned[...], back[...].reshape(inverse.shape[0], -1))
        middle[...] = total
        unit, factor = norm_forward(total)
        units[...] = unit
        factors[...] = jnp.broadcast_to(factor, factors.shape)
        tokens[...] = (unit * vectors[2:3, :] + vectors[3:4, :]).astype(BF16)
        grad_low[...] = only(mask, cotangent[...].astype(F32)).astype(BF16)
        lower[...] = jnp.zeros_like(lower)
        grad_tokens[...] = jnp.zeros_like(grad_tokens)

    @pl.when((step == 0) & (pl.program_id(0) == 0))
    def _():
        sums[...] = jnp.zeros_like(sums)

    dots = [
        (dot_nt(tokens[...], half[0]), dot_nt(grad_low[...], half[1])) for half in (mine, other)
    ]
    values, grads = [], []
    for half, (upper_in, grad_hidden) in enumerate(dots):
        value, slope = gelu_pair(upper_in + hidden_bias[half])
        grad_upper = grad_hidden * slope
        values.append(value.astype(BF16))
        grads.append(grad_upper.astype(BF16))
        hidden[half] = values[half]
        upper[half] = grads[half]
        upper_sums[half] = jnp.sum(grad_upper, axis=0, keepdims=True)

    def joined(parts, axis):
        return jnp.concatenate(parts, axis=axis)

    lower[...] += dot(joined(values, 1), joined([mine[1], other[1]], 0))
    grad_tokens[...] += dot(joined(grads, 1), joined([mine[0], other[0]], 0))

    @pl.when(step == steps - 1)
    def _():
        total = middle[...]
        output[...] = only(mask, total + lower[...] + vectors[8:9, :]).astype(BF16)
        unit, factor = units[...], factors[:, 0:1]
        grad = grad_tokens[...]
        grad_out = grad_low[...].astype(F32)
        sums[0:1, :] += jnp.sum(grad * unit, axis=0, keepdims=True)
        sums[1:2, :] += jnp.sum(grad, axis=0, keepdims=True)
        sums[2:3, :] += jnp.sum(grad_out, axis=0, keepdims=True)
        through = grad_out + norm_backward(grad, unit, factor, vectors[2:3, :])
        middle[...] = through
        turned = dot(inverse[...], through.astype(BF16))
        grad_back[...] = turned.astype(BF16).reshape(grad_back.shape)


def weight_grad_kernel(groups, *refs):
    up, down = None, None
    for g in range(groups):
        hidden, upper, tokens, grad_low = refs[4 * g : 4 * g + 4]

        def flat(ref):
            return ref[...].reshape(-1, ref.shape[-1])

        up_part = dot_tn(flat(upper), flat(tokens))
        down_part = dot_tn(flat(hidden), flat(grad_low))
        up = up_part if up is None else up + up_part
        down = down_part if down is None else down + down_part
    rest = refs[4 * groups :]
    if len(rest[-1].shape) == 2:
        rest[-2][...] = up.astype(BF16)
        rest[-1][...] = down.astype(BF16)
    else:
        blocks, _, units, features = rest[-1].shape
        for part, grads in enumerate((up, down)):
            grads = grads + rest[part][...].astype(F32)
            rest[-1][:, part] = grads.astype(BF16).reshape(blocks, units, features)


def pack_kernel(early, dense_raw, own, *rest):
    out = rest[-1]
    out[...] = early[...]
    first = rest[0][0:2, :]
    for sums in rest[1:-1]:
        first = first + sums[0:2, :]
    out[0:2, :] = first
    squares = jnp.square(dense_raw[0].astype(F32)) + jnp.square(dense_raw[1].astype(F32))
    out[13:14, :] = jnp.sum(squares, axis=0, keepdims=True)
    out[14:15, 0:BS] = jnp.sum(jnp.square(own[...]), axis=0, keepdims=True)


def input_kernel(first, limits, patches, spread, table_turned, vectors, grad_middle, *rest):
    out, sums = rest[-2:]
    count = limits[first + pl.program_id(0)]
    mask = valid_rows(count, patches.shape[0])

    @pl.when(pl.program_id(0) == 0)
    def _():
        sums[...] = jnp.zeros_like(sums)

    unit, factor = norm_forward(only(mask, patches[...].astype(F32)))
    through = grad_middle[...]
    narrow = dot(table_turned[...], spread[...].reshape(table_turned.shape[1], -1))
    grad_normed = only(mask, through + narrow)
    sums[0:1, :] += jnp.sum(grad_normed * unit, axis=0, keepdims=True)
    sums[1:2, :] += jnp.sum(grad_normed, axis=0, keepdims=True)
    start = through + norm_backward(grad_normed, unit, factor, vectors[0:1, :])
    out[...] = only(mask, start).astype(BF16)


def update_kernel(halves, late, *refs):
    dense_raw, dense_old, refs = refs[0], refs[1:4], refs[4:]
    spectral_raw, refs = refs[:halves], refs[halves:]
    spectral_old, vector_old, refs = refs[0:3], refs[3:6], refs[6:]
    norm, dense_out, spectral_out, vector_out = refs[0], refs[1:5], refs[5:9], refs[9:13]
    vector_raw = late[0:13, :]
    squares = jnp.sum(vector_raw * vector_raw, axis=1, keepdims=True)
    squares = jnp.sum(squares, axis=0, keepdims=True)
    for row in (13, 14):
        squares = squares + jnp.sum(late[row : row + 1, :], axis=1, keepdims=True)
    grad_norm = jnp.sqrt(squares)
    factor = jnp.minimum(1.0, CLIP_LEVEL / (grad_norm + 1e-06))
    norm[...] = grad_norm

    def update(raw, old, out, at, rate, decay):
        grad = raw.astype(F32) * factor.reshape((1,) * raw.ndim)
        news = adam_update(*(ref[at] for ref in old), grad, rate, decay)
        for ref, value in zip(out, (grad,) + news):
            ref[at] = value

    for part in range(2):
        at = (slice(None), part, slice(None))
        update(dense_raw[part], dense_old, dense_out, at, RATE_MATRIX, DECAY_MATRIX)
    if halves == 1:
        update(spectral_raw[0][...], spectral_old, spectral_out, ..., RATE_MATRIX, DECAY_MATRIX)
    else:
        core = lax.axis_index("modes") % 2
        for half, raw in enumerate(spectral_raw):
            for z in range(raw.shape[0]):
                at = pl.ds(2 * z + (core ^ half), 1)
                update(raw[z : z + 1], spectral_old, spectral_out, at, RATE_MATRIX, DECAY_MATRIX)

    @pl.when(pl.program_id(0) == 0)
    def _():
        update(vector_raw, vector_old, vector_out, ..., RATE_VECTOR, 0.0)


def update_call(late, dense_raw, dense_old, spectral_raw, spectral_old, vector_old):
    steps = 4
    units, _, features = dense_old[0].shape
    spectral_shape = spectral_old[0].shape
    spectral_old = [old.reshape(32, BS, BS) for old in spectral_old]
    dense = pl.BlockSpec((units // steps, 2, features), lambda i: (i, 0, 0))
    raw = pl.BlockSpec((2, units // steps, features), lambda i: (0, i, 0))
    if units // steps % 8:
        raw = dense = None
    if dense is None:
        dense, raw = whole(dense_old[0]), whole(dense_raw)
    spectral = pl.BlockSpec((8, BS, BS), lambda i: (i, 0, 0))
    blocks = spectral_raw[0].shape[1]
    sums = pl.BlockSpec((None, blocks, BS, BS), lambda i: (i, 0, 0, 0))
    vector = whole(vector_old[0])
    out = pl.pallas_call(
        functools.partial(update_kernel, len(spectral_raw)),
        grid=(steps,),
        in_specs=[whole(late), raw]
        + [dense] * 3
        + [sums] * len(spectral_raw)
        + [spectral] * 3
        + [vector] * 3,
        out_specs=[pl.BlockSpec((1, 1), lambda i: (0, 0))]
        + [dense] * 4
        + [spectral] * 4
        + [vector] * 4,
        out_shape=[
            jax.ShapeDtypeStruct(shape, F32)
            for shape in [(1, 1)]
            + [dense_old[0].shape] * 4
            + [(32, BS, BS)] * 4
            + [vector_old[0].shape] * 4
        ],
        compiler_params=params(),
        cost_estimate=cost(0, 32 * (dense_raw.size + 32 * BS * BS)),
        name="update",
    )(late, dense_raw, *dense_old, *spectral_raw, *spectral_old, *vector_old)
    spectral_new = [new.reshape(spectral_shape) for new in out[5:9]]
    return (out[0].reshape(()), *out[1:5], *spectral_new, *out[9:13])


def split_blocks(values):
    return values.reshape(values.shape[:-1] + (NB, BS))


def block_mix(values, matrix):
    mixed = jnp.einsum(
        "ckpsni,pqnij->ckqsnj", split_blocks(values), matrix, preferred_element_type=F32
    )
    return mixed.reshape(values.shape)


def complex_matrix(weights):
    return jnp.stack([jnp.stack([weights[0], weights[1]]), jnp.stack([-weights[1], weights[0]])])


def fold_complex(grad_matrix):
    return jnp.stack([grad_matrix[0, 0] + grad_matrix[1, 1], grad_matrix[0, 1] - grad_matrix[1, 0]])


def shrink(values):
    return values - SHRINK_LEVEL * jnp.tanh(values / SHRINK_LEVEL)


def plain_filter(received, mixes, biases, keep, tables):
    band_count, crops, rows, features = received.shape
    rows_in = received.reshape(band_count, crops, 2, rows // 2, features)
    modes = jnp.einsum("pjqh,hcqsd->cjpsd", tables[0], rows_in, preferred_element_type=F32)
    modes = modes.astype(BF16)
    pre_active = block_mix(modes, mixes[0]) + biases[0]
    active = jax.nn.gelu(pre_active).astype(BF16)
    pre_shrink = block_mix(active, mixes[1]) + biases[1]
    shrunk = (shrink(pre_shrink) * keep).astype(BF16)
    back = jnp.einsum("phqj,cjqsd->hcpsd", tables[1], shrunk, preferred_element_type=F32)
    return ((modes, pre_active, pre_shrink), back.astype(BF16).reshape(received.shape))


def plain_filter_back(received, saved, mixes, keep, tables):
    modes, pre_active, pre_shrink = saved
    band_count, crops, rows, features = received.shape
    grads = received.reshape(band_count, crops, 2, rows // 2, features)
    grad_shrunk = jnp.einsum("phqj,hcpsd->cjqsd", tables[1], grads, preferred_element_type=F32)
    grad_shrink = jax.vjp(shrink, pre_shrink)[1](grad_shrunk * keep)[0]
    shrink_low = grad_shrink.astype(BF16)
    active_value, active_pull = jax.vjp(jax.nn.gelu, pre_active)
    pairs = "chpsni,chqsnm->pqnim"
    grad_second = jnp.einsum(
        pairs,
        split_blocks(active_value.astype(BF16)),
        split_blocks(shrink_low),
        preferred_element_type=F32,
    )
    back = "cjqsnk,pqnik->cjpsni"
    grad_active = jnp.einsum(
        back, split_blocks(shrink_low), mixes[1], preferred_element_type=F32
    ).reshape(pre_active.shape)
    grad_first = active_pull(grad_active)[0]
    first_low = grad_first.astype(BF16)
    grad_one = jnp.einsum(
        pairs, split_blocks(modes), split_blocks(first_low), preferred_element_type=F32
    )
    grad_modes = jnp.einsum(
        back, split_blocks(first_low), mixes[0], preferred_element_type=F32
    ).reshape(pre_active.shape)
    spread = jnp.einsum(
        "pjqh,cjpsd->hcqsd", tables[0], grad_modes.astype(BF16), preferred_element_type=F32
    )
    weights = jnp.stack([fold_complex(grad_one), fold_complex(grad_second)])
    sums = jnp.concatenate(
        [jnp.sum(grad_first, axis=(0, 1, 3)), jnp.sum(grad_shrink, axis=(0, 1, 3))]
    )
    return (spread.astype(BF16).reshape(received.shape), weights, sums)


def on_device(
    patches,
    cotangent,
    heights,
    widths,
    band_lengths,
    dense_master,
    dense_first,
    dense_second,
    spectral_master,
    spectral_first,
    spectral_second,
    vector_master,
    vector_first,
    vector_second,
):
    band_count = lax.axis_size("modes")
    my_band = lax.axis_index("modes")
    micros = patches.shape[0]
    cells, features = patches.shape[3:]
    wave_count = cells // 2
    slots = wave_count // band_count
    rows = 2 * slots
    hidden_units = 4 * features
    direct = band_count == 8 and slots % 16 == 0
    groups = [[0, 1], [2, 3]] if micros == 4 else [[m] for m in range(micros)]
    spans = features // SPAN

    kept_count = jnp.minimum(jnp.sum(band_lengths), wave_count)
    counts = jnp.where(my_band < heights[:, 0], widths[:, 0], 0)
    limits = jnp.concatenate(
        [counts, jnp.stack([my_band * slots, kept_count]).astype(jnp.int32)]
    ).astype(jnp.int32)
    forward, forward_turned, inverse, inverse_turned = wave_tables(band_count, cells)

    core = my_band % 2
    core_groups = [list(range(c, band_count, 2)) for c in range(2)]
    four = band_count == 8 and lax.axis_size("dp") == 4
    mine = dense_master.transpose(1, 0, 2).astype(BF16)
    mine = lax.all_gather(mine, "modes", axis=1, tiled=True, axis_index_groups=core_groups)
    half_units = hidden_units // 2

    def by_core(values, back=False):
        units = dense_master.shape[0]
        if back:
            values = jnp.where(core == 0, values, values[::-1]).reshape(2, -1, units)
            return values.transpose(1, 0, 2).reshape(-1)
        values = values.reshape(-1, 2, units).transpose(1, 0, 2).reshape(2, 1, half_units)
        return jnp.where(core == 0, values, values[::-1])

    hidden_bias = by_core(vector_master[9:13].reshape(-1))

    def exchange(values):
        return lax.all_to_all(values, "modes", split_axis=0, concat_axis=0, tiled=True)

    def micro_spec(group):
        return pl.BlockSpec(
            (None, None, None, cells, features), lambda g, *_: (group[0] + g, 0, 0, 0, 0)
        )

    def sent(group):
        if direct:
            return (
                jax.ShapeDtypeStruct((band_count, len(group), rows, features), BF16),
                pl.BlockSpec((band_count, None, rows, features), lambda g, *_: (0, g, 0, 0)),
            )
        return (
            jax.ShapeDtypeStruct((len(group), cells, features), BF16),
            pl.BlockSpec((None, cells, features), lambda g, *_: (g, 0, 0)),
        )

    def to_wire(values):
        if direct:
            return values
        return values.reshape(-1, band_count, rows, features).transpose(1, 0, 2, 3)

    def from_wire(values):
        if direct:
            return values
        return values.transpose(1, 0, 2, 3).reshape(-1, cells, features)

    matmul_flops = 2 * cells * cells * features
    cell_bytes = cells * features

    def spread_call(group):
        shape, spec = sent(group)
        per_micro = pl.BlockSpec((None, cells, features), lambda g: (g, 0, 0))
        out, base = pl.pallas_call(
            functools.partial(spread_kernel, group[0]),
            grid=(len(group),),
            in_specs=[SMEM, SMEM, micro_spec(group), whole(forward), whole(vector_master)],
            out_specs=[spec, per_micro],
            out_shape=[shape, jax.ShapeDtypeStruct((len(group), cells, features), F32)],
            compiler_params=params(),
            cost_estimate=cost(len(group) * matmul_flops, len(group) * 8 * cell_bytes),
            name="spread_rows",
        )(heights.reshape(-1), widths.reshape(-1), patches, forward, vector_master)
        return (to_wire(out), base)

    if direct:
        mixes = pl.pallas_call(
            mix_kernel,
            grid=(2,),
            in_specs=[pl.BlockSpec((None, 2, NB, BS, BS), lambda i: (i, 0, 0, 0, 0))],
            out_specs=pl.BlockSpec((None, spans, 2 * SPAN, 2 * SPAN), lambda i: (i, 0, 0, 0)),
            out_shape=jax.ShapeDtypeStruct((2, spans, 2 * SPAN, 2 * SPAN), BF16),
            compiler_params=params(SMALL),
            cost_estimate=cost(0, 16 * NB * BS * BS * 4),
            name="build_mix",
        )(spectral_master)
        biases = vector_master[4:8].reshape(2, 2, spans, SPAN).transpose(0, 2, 1, 3)
        biases = biases.reshape(2, spans, 1, 2 * SPAN)
    else:
        low = spectral_master.astype(BF16)
        mixes = (complex_matrix(low[0]), complex_matrix(low[1]))
        biases = (
            vector_master[4:6][None, None, :, None, :],
            vector_master[6:8][None, None, :, None, :],
        )
        tables = row_tables(band_count)
        keep = (my_band * slots + jnp.arange(slots, dtype=jnp.int32) < kept_count).astype(F32)
        keep = keep[None, None, None, :, None]
    mode_rows = 8 * slots
    mix_flops = 2 * mode_rows * (2 * SPAN) * (2 * SPAN) * spans

    def filter_call(group, received):
        if not direct:
            return plain_filter(received, mixes, biases, keep, tables)
        shape, _ = sent(group)
        saved = jax.ShapeDtypeStruct((spans, len(group) * mode_rows, 2 * SPAN), BF16)
        modes, back = pl.pallas_call(
            functools.partial(filter_kernel, slots, micros),
            in_specs=[SMEM, VMEMS, VMEMS, VMEMS],
            out_shape=[saved, shape],
            scratch_shapes=[pltpu.VMEM(saved.shape, BF16)],
            compiler_params=params(),
            cost_estimate=cost(len(group) * 2 * mix_flops, len(group) * 6 * cell_bytes),
            name="filter_modes",
        )(limits, received, mixes, biases)
        return (modes, back)

    def filter_back_call(group, received, saved, ahead, before):
        if not direct:
            return plain_filter_back(received, saved, mixes, keep, tables)
        shape, _ = sent(group)
        blocks = jax.ShapeDtypeStruct((4, 4, BS, BS), F32)
        spread, sums, mine, other = pl.pallas_call(
            lambda *refs: filter_back_kernel(slots, micros, *refs[: 5 + len(before)], *refs[6 + len(before) :]),
            in_specs=[SMEM] + [VMEMS] * (4 + len(before)) + [HBM],
            out_shape=[
                shape,
                jax.ShapeDtypeStruct((spans, 8, 2 * SPAN), F32),
                blocks,
                blocks,
            ],
            scratch_shapes=[
                pltpu.VMEM((2, spans, 2 * SPAN, 2 * SPAN), F32),
                pltpu.VMEM((spans, len(group) * mode_rows, 2 * SPAN), F32),
            ],
            compiler_params=params(),
            cost_estimate=cost(1 + len(before) * 10**11, 1),
            name="filter_modes_back",
        )(limits, received, saved, mixes, biases, *before, ahead)
        sums = sums[:, 0:2].reshape(spans, 2, 2, SPAN).transpose(1, 2, 0, 3).reshape(4, features)
        return (spread, (mine, other), sums)

    tile = 512

    def dense_call(group, base, back, output):
        shape, spec = sent(group)
        count = len(group)
        per_micro = pl.BlockSpec((None, cells, features), lambda g, t: (g, 0, 0))
        per_tile = pl.BlockSpec((2, None, cells, tile), lambda g, t: (0, g, 0, t))
        per_half = pl.BlockSpec((2, tile, features), lambda g, t: (0, t, 0))
        previous = [] if output is None else [output]
        operands = [
            limits,
            base,
            cotangent,
            back,
            inverse_turned,
            inverse,
            vector_master,
            hidden_bias,
            mine,
            other,
        ]
        whole_low = jax.ShapeDtypeStruct((count, cells, features), BF16)
        whole_full = jax.ShapeDtypeStruct((count, cells, features), F32)
        sums = jax.ShapeDtypeStruct((8, features), F32)
        tiled = jax.ShapeDtypeStruct((2, count, cells, half_units), BF16)
        return pl.pallas_call(
            functools.partial(dense_kernel, group[0]),
            grid=(count, half_units // tile),
            in_specs=[
                SMEM,
                per_micro,
                micro_spec(group),
                spec,
                whole(inverse_turned),
                whole(inverse),
                whole(vector_master),
                pl.BlockSpec((2, 1, tile), lambda g, t: (0, 0, t)),
                per_half,
                per_half,
            ]
            + [ANY for _ in previous],
            out_specs=[
                micro_spec(group),
                per_tile,
                per_tile,
                per_micro,
                per_micro,
                spec,
                per_micro,
                whole(sums),
                pl.BlockSpec((2, None, 1, tile), lambda g, t: (0, g, 0, t)),
            ],
            out_shape=[
                jax.ShapeDtypeStruct(patches.shape, BF16),
                tiled,
                tiled,
                whole_low,
                whole_low,
                shape,
                whole_full,
                sums,
                jax.ShapeDtypeStruct((2, count, 1, half_units), F32),
            ],
            scratch_shapes=[pltpu.VMEM((cells, features), F32) for _ in range(3)]
            + [pltpu.VMEM((cells, LANES), F32)],
            input_output_aliases={len(operands): 0} if previous else {},
            compiler_params=params(),
            cost_estimate=cost(
                count * 8 * cells * features * hidden_units,
                count * (20 * cell_bytes + 4 * cells * hidden_units)
                + 4 * features * hidden_units * count,
            ),
            name="dense_both_ways",
        )(*operands, *previous)

    chunk = half_units // 4
    own_units = dense_master.shape[0]

    def weight_grad_call(saved, half, received, ahead):
        specs, operands = [], []
        for hidden, upper, tokens, grad_low in saved:
            per_chunk = pl.BlockSpec(
                (None, hidden.shape[1], cells, chunk), lambda t: (half, 0, 0, t)
            )
            specs += [per_chunk, per_chunk, whole(tokens), whole(grad_low)]
            operands += [hidden, upper, tokens, grad_low]
        single = pl.BlockSpec((chunk, features), lambda t: (t, 0))
        out_specs = [single] * 2
        out_shape = [jax.ShapeDtypeStruct((half_units, features), BF16)] * 2
        if received:
            owners = chunk // own_units
            out_specs = pl.BlockSpec((owners, 2, own_units, features), lambda t: (t, 0, 0, 0))
            out_shape = jax.ShapeDtypeStruct((4 * owners, 2, own_units, features), BF16)
        return pl.pallas_call(
            functools.partial(weight_grad_kernel, len(saved)),
            grid=(4,),
            in_specs=specs + [single] * len(received) + [ANY] * len(ahead),
            out_specs=out_specs,
            out_shape=out_shape,
            compiler_params=params(),
            cost_estimate=cost(1, 1 if received else 16 * micros * cell_bytes),
            name="dense_weight_grads",
        )(*operands, *received, *ahead)

    def input_call(group, spread, grad_middle, input_grad, ahead):
        _, spec = sent(group)
        previous = [] if input_grad is None else [input_grad]
        operands = [limits, patches, spread, forward_turned, vector_master, grad_middle]
        operands += ahead
        return pl.pallas_call(
            functools.partial(input_kernel, group[0]),
            grid=(len(group),),
            in_specs=[
                SMEM,
                micro_spec(group),
                spec,
                whole(forward_turned),
                whole(vector_master),
                pl.BlockSpec((None, cells, features), lambda g: (g, 0, 0)),
            ]
            + [HBM for _ in ahead]
            + [ANY for _ in previous],
            out_specs=[micro_spec(group), pl.BlockSpec((8, features), lambda g: (0, 0))],
            out_shape=[
                jax.ShapeDtypeStruct(patches.shape, BF16),
                jax.ShapeDtypeStruct((8, features), F32),
            ],
            input_output_aliases={len(operands): 0} if previous else {},
            compiler_params=params(),
            cost_estimate=cost(len(group) * matmul_flops, len(group) * 11 * cell_bytes),
            name="input_grads",
        )(*operands, *previous)

    def exchange_all(values):
        done = []
        for value, others in values:
            done.append(exchange(tie(value, *done[-1:], *others) if done or others else value))
        return done

    spread, bases = zip(*[spread_call(group) for group in groups])
    received = exchange_all([(values, ()) for values in spread])
    mine = lax.all_gather(tie(mine, received[0], spread[1]), "dp", axis=1, tiled=True)
    filtered = [filter_call(group, got) for group, got in zip(groups, received)]
    returned = exchange_all([(back, received[-1:]) for _, back in filtered])
    mine = tie(mine, returned[0], jax.tree.leaves(filtered[-1][0])[0])
    other = swap(mine, "modes", 1)
    output, dense_parts = None, []
    for group, back, base in zip(groups, returned, bases):
        dense_parts.append(dense_call(group, base, from_wire(back), output))
        output = dense_parts[-1][0]
    received = exchange_all([(to_wire(part[5]), returned[-1:]) for part in dense_parts])
    saved_parts = [part[1:5] for part in dense_parts]
    turned, ahead = [], received[0]
    for group, got, (saved, _) in zip(groups, received, filtered):
        before = turned[-1][1] if turned and direct else ()
        turned.append(filter_back_call(group, got, saved, ahead, before))
        if len(turned) == 1:
            other_grads = weight_grad_call(saved_parts, 1, (), jax.tree.leaves(turned[0][1])[:1])
            other_grads = [swap(grads, "modes", 1) for grads in other_grads]
            after = [received[-1], jax.tree.leaves(turned[0][1])[0]]
            dense_raw = weight_grad_call(saved_parts, 0, other_grads, after)
            ahead = dense_raw
    returned = exchange_all([(part[0], (received[-1],)) for part in turned])
    dense_raw = lax.psum_scatter(dense_raw, "dp", scatter_dimension=0, tiled=True)
    dense_sums = sum(part[7] for part in dense_parts)
    early = jnp.concatenate(
        [
            jnp.zeros((2, features), F32),
            dense_sums[0:2],
            sum(part[2] for part in turned),
            dense_sums[2:3],
            by_core(sum(jnp.sum(part[8], axis=1) for part in dense_parts), True).reshape(-1, features),
            jnp.zeros((3, features), F32),
        ]
    )

    input_grad, input_sums = None, []
    if four:
        spectral_parts = scatter_spectral(*turned[-1][1])
        spectral_own = own_spectral(spectral_parts)
    else:
        spectral_parts = returned
    for group, spread, part in zip(groups, returned, dense_parts):
        ahead = [spectral_own] if four and group == groups[-1] else [early]
        input_grad, sums = input_call(group, from_wire(spread), part[6], input_grad, ahead)
        input_sums.append(sums)
    dense_raw = lax.psum_scatter(
        tie(dense_raw, returned[-1], input_sums[0], spectral_parts[-1]),
        "modes",
        scatter_dimension=0,
        tiled=True,
        axis_index_groups=core_groups,
    )[0]
    def pack(own):
        return pick_call(
            pack_kernel,
            jax.ShapeDtypeStruct(early.shape, F32),
            early,
            dense_raw,
            own,
            *input_sums,
            name="pack_sums",
        )

    if four:
        spectral_sum = gather_spectral(spectral_own, input_sums[-1])
        late = pack(tie(spectral_own, spectral_sum[0]))
        late = late + swap(late, "modes", 1)
        late = sum_four(late, "dp", 1)
        late = sum_four(late, "modes", 2)
    else:
        if direct:
            even, odd = (jnp.where(core == c, *turned[-1][1]) for c in range(2))
            spectral_raw = jnp.stack([even, odd], axis=2)
        else:
            spectral_raw = sum(part[1] for part in turned)
        spectral_sum = [lax.psum(spectral_raw, ("dp", "modes")).reshape(4, 8, BS, BS)]
        late = pack(jnp.zeros((BS, BS), F32))
        late = lax.psum(late, ("dp", "modes"))
        squares = jnp.sum(spectral_sum[0] * spectral_sum[0])
        late = jnp.concatenate([late[:15], jnp.zeros((1, features), F32)]).at[14].add(squares / features)
    updated = update_call(
        late,
        dense_raw,
        (dense_master, dense_first, dense_second),
        spectral_sum,
        (spectral_master, spectral_first, spectral_second),
        (vector_master, vector_first, vector_second),
    )
    return (output, input_grad) + updated


def solution(mesh):
    return jax.shard_map(
        on_device,
        mesh=mesh,
        in_specs=(
            P(None, "dp", "modes", None, None),
            P(None, "dp", "modes", None, None),
            P(None, "dp"),
            P(None, "dp"),
            P(),
            P(("dp", "modes"), None, None),
            P(("dp", "modes"), None, None),
            P(("dp", "modes"), None, None),
            P(),
            P(),
            P(),
            P(),
            P(),
            P(),
        ),
        out_specs=(
            P(None, "dp", "modes", None, None),
            P(None, "dp", "modes", None, None),
            P(),
            P(("dp", "modes"), None, None),
            P(("dp", "modes"), None, None),
            P(("dp", "modes"), None, None),
            P(("dp", "modes"), None, None),
            P(),
            P(),
            P(),
            P(),
            P(),
            P(),
            P(),
            P(),
        ),
        check_vma=False,
    )
```
